256 devices in a mesh: dp: 32 (over x, y, z_hi), fsdp: 8 (over z_lo, core).
Axes of the slice: x: 4, y: 4, z: 8 (z_hi: 2, z_lo: 4; z = z_hi * 4 + z_lo), core: 2. Of those that a mesh axis runs over, the one named last changes fastest.
Arguments:
- acts: bfloat16 [32768, 7168], P('dp', 'fsdp'), may hold values from -6 to 6
- out_grads: bfloat16 [32768, 12288], P('dp'), may hold values from -0.0625 to 0.0625
- basis: bfloat16 [7168, 512], P('fsdp'), may hold values from -0.0625 to 0.0625
- weight: bfloat16 [7168, 12288], P('fsdp', 'dp'), may hold values from -6 to 6
- first_moment: float32 [512, 12288], P('fsdp', 'dp'), may hold values from -0.3 to 0.3
- second_moment: float32 [512, 12288], P('fsdp', 'dp'), may hold values from 0.002 to 0.02
Outputs:
- new_weight: bfloat16 [7168, 12288], P(None, 'dp')
- new_first: float32 [512, 12288], P('fsdp', 'dp')
- new_second: float32 [512, 12288], P('fsdp', 'dp')
The draws below stay inside these ranges and needn't reach their ends.
All inputs are finite; a program needn't handle non-finite values.
Results may differ from the reference program's by a relative error of at most 0.0049.
Values may be sent and summed in bfloat16 or wider, within the bound.
No kernel may reach another device: no remote copies, remote signals or barrier semaphores. Data moves between devices by JAX's collectives and lax.ppermute only.
A program may use at most 128 MiB of HBM per device.

```python
import math
import jax
import jax.numpy as jnp

D = 7168
FF = 12288
RANK = 512
TOK_DEV = 1024
TOKENS = 32768
N_DP = 32


def strengthened(entries, rng, source, target, blocks, factor):
    owner, partner = [(jnp.arange(entries.shape[axis_at]) // (entries.shape[axis_at] // blocks)).reshape([-1 if axis == axis_at else 1 for axis in range(entries.ndim)]) for axis_at in (source, target)]
    chosen = jax.random.permutation(rng, blocks)[partner]
    strong = (owner == chosen) | (owner == (partner + blocks // 2) % blocks)
    return jnp.where(strong, factor * entries, entries)


def block_levels(stream_key, dims, shards, smallest, top_value):
    def one(axis_at, shards_of):
        heights = jax.random.uniform(jax.random.fold_in(jax.random.fold_in(stream_key, 6), axis_at), (shards_of,), jnp.float32, smallest / len(shards), top_value / len(shards))
        return jnp.repeat(jnp.exp(heights), dims[axis_at] // shards_of).reshape((-1,) + (1,) * (len(dims) - axis_at - 1))

    factor_of = one(*shards[0])
    for cut in shards[1:]:
        factor_of = factor_of * one(*cut)
    return factor_of


def normal_values(own_key, extent, width, bound, split=(), kind=jnp.bfloat16):
    entries = width * jax.random.normal(own_key, extent, jnp.float32)
    if split:
        entries = entries * block_levels(own_key, extent, split, -0.22, 0.18)
    return jnp.clip(entries, -bound, bound).astype(kind)


def heavy_noise(key, extent, scale, bound, shards, heavy, kind=jnp.bfloat16):
    entries = scale * jax.random.normal(key, extent, jnp.float32)
    if shards:
        entries = entries * block_levels(key, extent, shards, -0.22, 0.18)
    return jnp.clip(strengthened(entries, jax.random.fold_in(key, 3), *heavy), -bound, bound).astype(kind)


def setup_inputs(seed: int = 0) -> dict:
    seeds = jax.random.split(jax.random.key(seed), 7)
    return {
        "acts": normal_values(seeds[0], (TOKENS, D), 1.0, 6.0, ((0, 32), (1, 8))),
        "out_grads": heavy_noise(seeds[1], (TOKENS, FF), (TOK_DEV * N_DP) ** -0.5, 0.0625, ((0, 32),), (0, 1, 32, 2.75)),
        "basis": normal_values(seeds[2], (D, RANK), D ** -0.5, 0.0625, ((0, 8),)),
        "weight": normal_values(seeds[3], (D, FF), 1.0, 6.0, ((0, 8), (1, 32))),
        "first_moment": normal_values(seeds[4], (RANK, FF), 0.05, 0.3, ((0, 8), (1, 32)), jnp.float32),
        "second_moment": jnp.clip(jnp.exp(math.log(0.02) - 2.30258502 * jax.random.uniform(seeds[5], (RANK, FF), jnp.float32) ** block_levels(seeds[5], (RANK, FF), ((0, 8), (1, 32)), -0.2, 0.2)), 0.002, 0.02),
    }


first_fix = 0.99997343860111
second_fix = 0.0952078528

def reference(acts, out_grads, basis, weight, first_moment, second_moment):
    projected = jnp.dot(acts, basis, preferred_element_type=jnp.float32).astype(jnp.bfloat16)
    grad = jnp.dot(projected.T, out_grads, preferred_element_type=jnp.float32)
    new_first = 0.9 * first_moment + 0.1 * grad
    new_second = 0.999 * second_moment + 0.001 * grad * grad
    direction = (new_first / first_fix / (jnp.sqrt(new_second / second_fix) + 1e-08)).astype(jnp.bfloat16)
    lifted = jnp.dot(basis, direction, preferred_element_type=jnp.float32)
    new_weight = (weight.astype(jnp.float32) - 8.0 * lifted).astype(jnp.bfloat16)
    return (new_weight, new_first, new_second)
```

```python
import jax
import jax.numpy as jnp
from jax import lax
from jax.experimental import pallas as pl
from jax.experimental.pallas import tpu as pltpu
from jax.sharding import Mesh, PartitionSpec as P

first_fix = 0.99997343860111
second_fix = 0.0952078528

DP = ("x", "y", "zh")
FSDP = ("zl", "core")
BF = jnp.bfloat16
F32 = jnp.float32


def grad_kernel(ranks_ref, grads_ref, out_ref):
    both = jnp.dot(ranks_ref[...], grads_ref[...], preferred_element_type=F32).astype(BF)
    half = out_ref.shape[-1]
    for i in range(2):
        out_ref[0, i] = both[:, i * half : (i + 1) * half]


def grad_blocks(ranks, out_grads, blocks):
    rank_local, tokens = ranks.shape
    width = out_grads.shape[1] // blocks
    return pl.pallas_call(
        grad_kernel,
        grid=(blocks // 2,),
        in_specs=[
            pl.BlockSpec((rank_local, tokens), lambda j: (0, 0)),
            pl.BlockSpec((tokens, 2 * width), lambda j: (0, j)),
        ],
        out_specs=pl.BlockSpec((1, 2, rank_local, width), lambda j: (j, 0, 0, 0)),
        out_shape=jax.ShapeDtypeStruct((blocks // 2, 2, rank_local, width), BF),
        compiler_params=pltpu.CompilerParams(vmem_limit_bytes=32 * 2**20),
        cost_estimate=pl.CostEstimate(
            flops=2 * rank_local * tokens * blocks * width,
            bytes_accessed=2 * tokens * blocks * width,
            transcendentals=0,
        ),
    )(ranks, out_grads)


def lift_kernel(where_ref, *refs):
    pieces, (mine_ref, other_ref, weight_ref, weight2_ref, out_ref, dirs) = refs[:4], refs[4:]
    core, zl = where_ref[0], where_ref[1]
    pair = pieces[0].shape[0]

    @pl.when(pl.program_id(0) == 0)
    def _():
        for r, piece in enumerate(pieces):
            at = lax.rem(zl - r + 4, 4) * pair
            dirs[pl.ds(pl.multiple_of(at, pair), pair), :] = piece[...]

    rows = weight_ref.shape[1]
    part = mine_ref.shape[3]
    for b_ref, w_ref, c in ((mine_ref, weight_ref, core), (other_ref, weight2_ref, 1 - core)):
        for x in range(4):
            block = jnp.concatenate([b_ref[x, y, 0] for y in range(4)], axis=-1)
            lifted = jnp.dot(block, dirs[...], preferred_element_type=F32)
            old = w_ref[0, x * part : (x + 1) * part, :].astype(F32)
            at = pl.multiple_of(c * rows + x * part, part)
            out_ref[pl.ds(at, part), :] = (old - 8.0 * lifted).astype(BF)


def lift(where, pieces, mine, other, weight_mine, weight_other):
    _, rows, width = weight_mine.shape
    pair = pieces[0].shape[0]
    part, lanes = mine.shape[3:]
    basis_spec = pl.BlockSpec((4, 4, 1, part, lanes), lambda i, w: (0, 0, i, 0, 0))
    weight_spec = pl.BlockSpec((1, rows, width), lambda i, w: (i, 0, 0))
    return pl.pallas_call(
        lift_kernel,
        grid_spec=pltpu.PrefetchScalarGridSpec(
            num_scalar_prefetch=1,
            grid=(4,),
            in_specs=[pl.BlockSpec((pair, width), lambda i, w: (0, 0))] * 4
            + [basis_spec] * 2
            + [weight_spec] * 2,
            out_specs=pl.BlockSpec((2 * rows, width), lambda i, w: (i, 0)),
            scratch_shapes=[pltpu.VMEM((4 * pair, width), BF)],
        ),
        out_shape=jax.ShapeDtypeStruct((8 * rows, width), BF),
        compiler_params=pltpu.CompilerParams(vmem_limit_bytes=32 * 2**20),
        cost_estimate=pl.CostEstimate(
            flops=2 * 8 * rows * 4 * pair * width,
            bytes_accessed=2 * 8 * rows * (2 * width + 4 * pair),
            transcendentals=0,
        ),
    )(where, *pieces, mine, other, weight_mine, weight_other)


def swap(value, axis):
    return lax.ppermute(value, axis, [(0, 1), (1, 0)])


def around(value, shift):
    return lax.ppermute(value, "zl", [(i, (i + shift) % 4) for i in range(4)])


def pick(value, at, axis=0):
    return lax.dynamic_index_in_dim(value, at, axis, keepdims=False)


def shards(acts, out_grads, basis, weight, first_moment, second_moment):
    rank_local, width = first_moment.shape
    rows, rank = basis.shape
    tokens = acts.shape[0]
    x, y, zh, zl, core = (lax.axis_index(a) for a in ("x", "y", "zh", "zl", "core"))

    with jax.named_scope("gather_ahead"):
        weight_mine = lax.all_gather(weight, "zl")
        tile = lax.dynamic_slice(basis, (x * (rows // 4), y * (rank // 4)), (rows // 4, rank // 4))
        tiles = lax.dynamic_update_index_in_dim(
            jnp.zeros((4,) + tile.shape, BF), tile, zl, 0
        )
        for r in range(1, 4):
            tiles = lax.dynamic_update_index_in_dim(
                tiles, around(tile, r), (zl - r) % 4, 0
            )
        mine = lax.all_gather(tiles, ("x", "y")).reshape((4, 4) + tiles.shape)
        other = swap(mine, "core")
        weight_other = swap(weight_mine, "core")

    with jax.named_scope("project"):
        partial_t = lax.dot_general(
            basis, acts, (((0,), (1,)), ((), ())), preferred_element_type=F32
        ).reshape(4, 2, rank_local, tokens)
        got = swap(pick(partial_t, 1 - core, 1).astype(BF), "core")
        mixed = pick(partial_t, core, 1) + got.astype(F32)
        total = pick(mixed, zl)
        for r in range(1, 4):
            total = total + around(pick(mixed, (zl + r) % 4).astype(BF), r).astype(F32)
        ranks_t = total.astype(BF)

    with jax.named_scope("grad"):
        blocks = grad_blocks(ranks_t, out_grads, 32)
        parts = lax.all_to_all(blocks, ("x", "y"), 0, 0)
        halves = jnp.sum(parts.astype(F32), axis=0)
        grad = pick(halves, zh) + swap(pick(halves, 1 - zh).astype(BF), "zh").astype(F32)

    with jax.named_scope("adam"):
        new_first = 0.9 * first_moment + 0.1 * grad
        new_second = 0.999 * second_moment + 0.001 * grad * grad
        direction = (
            new_first / first_fix / (jnp.sqrt(new_second / second_fix) + 1e-08)
        ).astype(BF)

    with jax.named_scope("lift"):
        theirs = swap(direction, "core")
        pair = jnp.where(
            core == 0,
            jnp.concatenate([direction, theirs]),
            jnp.concatenate([theirs, direction]),
        )
        pieces = [pair] + [around(pair, r) for r in range(1, 4)]
        where = jnp.stack([core, zl]).astype(jnp.int32)
        new_weight = lift(where, pieces, mine, other, weight_mine, weight_other)
    return (new_weight, new_first, new_second)


def solution(mesh):
    split = Mesh(mesh.devices.reshape(4, 4, 2, 4, 2), DP + FSDP)
    placed = (
        P(DP, FSDP),
        P(DP, None),
        P(FSDP, None),
        P(FSDP, DP),
        P(FSDP, DP),
        P(FSDP, DP),
    )
    return jax.shard_map(
        shards,
        mesh=split,
        in_specs=placed,
        out_specs=(P(None, DP), P(FSDP, DP), P(FSDP, DP)),
        check_vma=False,
    )
```

```python
import jax
import jax.numpy as jnp
from jax import lax
from jax.experimental import pallas as pl
from jax.experimental.pallas import tpu as pltpu
from jax.sharding import Mesh, PartitionSpec as P

first_fix = 0.99997343860111
second_fix = 0.0952078528

DP = ("x", "y", "zh")
FSDP = ("zl", "core")
BF = jnp.bfloat16
F32 = jnp.float32


def grad_kernel(where_ref, ranks_ref, grads_ref, out_ref):
    del where_ref
    product = jnp.dot(ranks_ref[...], grads_ref[...], preferred_element_type=F32).astype(BF)
    width = out_ref.shape[-1]
    for i in range(out_ref.shape[0]):
        out_ref[i] = product[:, i * width : (i + 1) * width]


def grad_blocks(target, ranks, out_grads, blocks, width):
    rank_local, tokens = ranks.shape
    step = 4
    count = blocks // step
    return pl.pallas_call(
        grad_kernel,
        grid_spec=pltpu.PrefetchScalarGridSpec(
            num_scalar_prefetch=1,
            grid=(count,),
            in_specs=[
                pl.BlockSpec((rank_local, tokens), lambda j, w: (0, 0)),
                pl.BlockSpec((tokens, step * width), lambda j, w: (0, w[0] * count + j)),
            ],
            out_specs=pl.BlockSpec((step, rank_local, width), lambda j, w: (j, 0, 0)),
        ),
        out_shape=jax.ShapeDtypeStruct((blocks, rank_local, width), BF),
        compiler_params=pltpu.CompilerParams(vmem_limit_bytes=60 * 2**20),
        cost_estimate=pl.CostEstimate(flops=1024, bytes_accessed=1024, transcendentals=0),
    )(target, ranks, out_grads)


def lift_kernel(where_ref, *refs):
    pieces, weights, rest = refs[:4], refs[4:8], refs[8:]
    basis_ref, (out_ref, dirs, old, sems) = rest[0], rest[-4:]
    zl = where_ref[1]
    step = pl.program_id(0)
    pair = pieces[0].shape[0]
    copies = [
        pltpu.make_async_copy(weights[i], old.at[i], sems.at[i]) for i in range(4)
    ]

    @pl.when(step == 0)
    def _():
        for copy in copies:
            copy.start()
        for r, piece in enumerate(pieces):
            at = lax.rem(zl - r + 4, 4) * pair
            dirs[pl.ds(pl.multiple_of(at, pair), pair), :] = piece[...]

    for r in range(4):

        @pl.when(step == r)
        def _():
            copies[r].wait()

    part = basis_ref.shape[3]
    for x in range(4):
        block = jnp.concatenate([basis_ref[x, y, 0] for y in range(4)], axis=-1)
        lifted = jnp.dot(block, dirs[...], preferred_element_type=F32)
        before = old[step, x * part : (x + 1) * part, :].astype(F32)
        out_ref[x * part : (x + 1) * part, :] = (before - 8.0 * lifted).astype(BF)


def lift(where, pieces, weights, basis, filled=None):
    rows, width = weights[0].shape
    pair = pieces[0].shape[0]
    part, lanes = basis.shape[3:]
    anywhere = pl.BlockSpec(memory_space=pl.ANY)
    extra = [] if filled is None else [filled]
    return pl.pallas_call(
        lift_kernel,
        grid_spec=pltpu.PrefetchScalarGridSpec(
            num_scalar_prefetch=1,
            grid=(4,),
            in_specs=[pl.BlockSpec((pair, width), lambda i, w: (0, 0))] * 4
            + [anywhere] * 4
            + [pl.BlockSpec((4, 4, 1, part, lanes), lambda i, w: (0, 0, i, 0, 0))]
            + [anywhere] * len(extra),
            out_specs=pl.BlockSpec(
                (rows, width), lambda i, w: (lax.rem(w[1] - i + 4, 4) * 2 + w[0], 0)
            ),
            scratch_shapes=[
                pltpu.VMEM((4 * pair, width), BF),
                pltpu.VMEM((4, rows, width), BF),
                pltpu.SemaphoreType.DMA((4,)),
            ],
        ),
        out_shape=jax.ShapeDtypeStruct((8 * rows, width), BF),
        input_output_aliases={} if filled is None else {10: 0},
        compiler_params=pltpu.CompilerParams(vmem_limit_bytes=56 * 2**20),
        cost_estimate=pl.CostEstimate(
            flops=8 * rows * 4 * pair * width,
            bytes_accessed=8 * rows * (2 * width + 4 * pair),
            transcendentals=0,
        ),
    )(where, *pieces, *weights, basis, *extra)


def swap(value, axis):
    return lax.ppermute(value, axis, [(0, 1), (1, 0)])


def around(value, shift, axis="zl"):
    return lax.ppermute(value, axis, [(i, (i + shift) % 4) for i in range(4)])


def pick(value, at, axis=0):
    return lax.dynamic_index_in_dim(value, at, axis, keepdims=False)


def after(value, *others):
    return lax.optimization_barrier((value, *others))


def shards(acts, out_grads, basis, weight, first_moment, second_moment):
    rank_local, width = first_moment.shape
    rows, rank = basis.shape
    tokens = acts.shape[0]
    x, y, zh, zl, core = (lax.axis_index(a) for a in ("x", "y", "zh", "zl", "core"))

    with jax.named_scope("gather_ahead"):
        tile = lax.dynamic_slice(basis, (x * (rows // 4), y * (rank // 4)), (rows // 4, rank // 4))
        tiles = [tile] + [around(tile, r) for r in range(1, 4)]
        first_hop = around(weight, 1)

    with jax.named_scope("project"):
        partial_t = lax.dot_general(
            basis, acts, (((0,), (1,)), ((), ())), preferred_element_type=F32
        ).reshape(4, 2, rank_local, tokens)
    partial_t, *tiles = after(partial_t, *tiles)
    with jax.named_scope("gather_ahead"):
        mine = lax.all_gather(jnp.stack(tiles), ("x", "y")).reshape((4, 4, 4) + tile.shape)
    with jax.named_scope("project"):
        got = swap(pick(partial_t, 1 - core, 1).astype(BF), "core")
        mixed = pick(partial_t, core, 1) + got.astype(F32)
        total = pick(mixed, zl)
        for r in range(1, 4):
            total = total + around(pick(mixed, (zl + r) % 4).astype(BF), r).astype(F32)
        ranks_t = total.astype(BF)

    ranks_t, first_hop, weight = after(ranks_t, first_hop, weight)
    with jax.named_scope("gather_ahead"):
        second_hop = around(first_hop, 1)
        others = [swap(weight, "core")]

    with jax.named_scope("grad"):
        sums = []
        for r in (2, 1, 3, 0):
            target = jnp.reshape((x + r) % 4, (1,)).astype(jnp.int32)
            blocks = grad_blocks(target, ranks_t, out_grads, 8, width)
            ranks_t, blocks = after(ranks_t, blocks)
            sums.append(around(blocks, r, "x") if r else blocks)
        over_x = sum(part.astype(F32) for part in sums).reshape(4, 2, rank_local, width)
    over_x, first_hop, second_hop, others[0] = after(over_x, first_hop, second_hop, others[0])
    with jax.named_scope("gather_ahead"):
        third_hop = around(second_hop, 1)
        others.append(swap(first_hop, "core"))
    with jax.named_scope("grad"):
        halves = pick(over_x, y)
        for r in range(1, 4):
            halves = halves + around(pick(over_x, (y + r) % 4).astype(BF), r, "y").astype(F32)
    halves, second_hop, others[1] = after(halves, second_hop, others[1])
    with jax.named_scope("gather_ahead"):
        others.append(swap(second_hop, "core"))
    with jax.named_scope("grad"):
        grad = pick(halves, zh) + swap(pick(halves, 1 - zh).astype(BF), "zh").astype(F32)

    with jax.named_scope("adam"):
        new_first = 0.9 * first_moment + 0.1 * grad
        new_second = 0.999 * second_moment + 0.001 * grad * grad
        direction = (
            new_first / first_fix / (jnp.sqrt(new_second / second_fix) + 1e-08)
        ).astype(BF)

    with jax.named_scope("lift"):
        theirs = swap(direction, "core")
        theirs, third_hop, mine, others[2] = after(theirs, third_hop, mine, others[2])
        pair = jnp.where(
            core == 0,
            jnp.concatenate([direction, theirs]),
            jnp.concatenate([theirs, direction]),
        )
        pieces = [pair] + [around(pair, r) for r in range(1, 4)]
        other = swap(mine, "core")
        others.append(swap(third_hop, "core"))
        hops = [weight, first_hop, second_hop, third_hop]
        where = jnp.stack([core, zl]).astype(jnp.int32)
        half_done = lift(where, pieces, hops, mine)
        where = jnp.stack([1 - core, zl]).astype(jnp.int32)
        new_weight = lift(where, pieces, others, other, half_done)
    return (new_weight, new_first, new_second)


def solution(mesh):
    split = Mesh(mesh.devices.reshape(4, 4, 2, 4, 2), DP + FSDP)
    placed = (
        P(DP, FSDP),
        P(DP, None),
        P(FSDP, None),
        P(FSDP, DP),
        P(FSDP, DP),
        P(FSDP, DP),
    )
    return jax.shard_map(
        shards,
        mesh=split,
        in_specs=placed,
        out_specs=(P(None, DP), P(FSDP, DP), P(FSDP, DP)),
        check_vma=False,
    )
```

```python
import jax
import jax.numpy as jnp
from jax import lax
from jax.experimental import pallas as pl
from jax.experimental.pallas import tpu as pltpu
from jax.sharding import Mesh, PartitionSpec as P

first_fix = 0.99997343860111
second_fix = 0.0952078528

DP = ("x", "y", "zh")
FSDP = ("zl", "core")
BF = jnp.bfloat16
F32 = jnp.float32


def grad_kernel(ranks_ref, grads_ref, out_ref):
    product = jnp.dot(ranks_ref[...], grads_ref[...], preferred_element_type=F32).astype(BF)
    width = out_ref.shape[-1]
    for i in range(out_ref.shape[0]):
        out_ref[i] = product[:, i * width : (i + 1) * width]


def grad_blocks(ranks, out_grads, width):
    rank_local, tokens = ranks.shape
    blocks = out_grads.shape[1] // width
    step = 8
    return pl.pallas_call(
        grad_kernel,
        grid=(blocks // step,),
        in_specs=[
            pl.BlockSpec((rank_local, tokens), lambda j: (0, 0)),
            pl.BlockSpec((tokens, step * width), lambda j: (0, j)),
        ],
        out_specs=pl.BlockSpec((step, rank_local, width), lambda j: (j, 0, 0)),
        out_shape=jax.ShapeDtypeStruct((blocks, rank_local, width), BF),
        compiler_params=pltpu.CompilerParams(vmem_limit_bytes=60 * 2**20),
        cost_estimate=pl.CostEstimate(
            flops=8 * rank_local * tokens * blocks * width,
            bytes_accessed=2 * tokens * blocks * width,
            transcendentals=0,
        ),
    )(ranks, out_grads)


def lift_kernel(where_ref, *refs):
    pieces, weights, bases, rest = refs[:4], refs[4:12], refs[12:26], refs[26:]
    out_ref, dirs, old, base, done, in_sems, out_sems = rest
    y, zl, core = (where_ref[i] for i in range(3))
    pair = pieces[0].shape[0]
    rows = old.shape[2]
    lanes = base.shape[3] // 4
    loads = []
    for k in range(2):
        plane, *columns = bases[7 * k : 7 * k + 7]
        for z in range(4):
            sources = [plane.at[z]] + [columns[2 * i + z // 2].at[z % 2] for i in range(3)]
            group = [pltpu.make_async_copy(weights[4 * k + z], old.at[k, z], in_sems.at[k, z, 4])]
            for q, source in enumerate(sources):
                group.append(
                    pltpu.make_async_copy(
                        source,
                        base.at[k, z, :, q * lanes : (q + 1) * lanes],
                        in_sems.at[k, z, q],
                    )
                )
            for copy in group:
                copy.start()
            loads.append(group)
    for r, piece in enumerate(pieces):
        at = lax.rem(y - zl + r + 4, 4) * pair
        dirs[pl.ds(pl.multiple_of(at, pair), pair), :] = piece[...]
    stores = []
    for k in range(2):
        for z in range(4):
            for copy in loads[4 * k + z]:
                copy.wait()
            lifted = jnp.dot(base[k, z], dirs[...], preferred_element_type=F32)
            done[k, z] = (old[k, z].astype(F32) - 8.0 * lifted).astype(BF)
            owner = core if k == 0 else 1 - core
            at = (lax.rem(zl - z + 4, 4) * 2 + owner) * rows
            copy = pltpu.make_async_copy(
                done.at[k, z],
                out_ref.at[pl.ds(pl.multiple_of(at, rows), rows)],
                out_sems.at[k, z],
            )
            copy.start()
            stores.append(copy)
    for copy in stores:
        copy.wait()


def lift(where, pieces, weights, bases):
    rows, width = weights[0].shape
    pair = pieces[0].shape[0]
    lanes = bases[0].shape[2]
    anywhere = pl.BlockSpec(memory_space=pl.ANY)
    return pl.pallas_call(
        lift_kernel,
        in_specs=[pl.BlockSpec(memory_space=pltpu.SMEM)]
        + [pl.BlockSpec(memory_space=pltpu.VMEM)] * 4
        + [anywhere] * 22,
        out_specs=anywhere,
        scratch_shapes=[
            pltpu.VMEM((4 * pair, width), BF),
            pltpu.VMEM((2, 4, rows, width), BF),
            pltpu.VMEM((2, 4, rows, 4 * lanes), BF),
            pltpu.VMEM((2, 4, rows, width), BF),
            pltpu.SemaphoreType.DMA((2, 4, 5)),
            pltpu.SemaphoreType.DMA((2, 4)),
        ],
        out_shape=jax.ShapeDtypeStruct((8 * rows, width), BF),
        compiler_params=pltpu.CompilerParams(vmem_limit_bytes=56 * 2**20),
        cost_estimate=pl.CostEstimate(
            flops=16 * rows * 4 * pair * width,
            bytes_accessed=16 * rows * (2 * width + 4 * pair),
            transcendentals=0,
        ),
    )(where, *pieces, *weights, *bases)


def swap(value, axis):
    return lax.ppermute(value, axis, [(0, 1), (1, 0)])


def around(value, shift, axis="zl"):
    return lax.ppermute(value, axis, [(i, (i + shift) % 4) for i in range(4)])


def along_z(value, shift):
    return lax.ppermute(value, ("zh", "zl"), [(i, (i + shift) % 8) for i in range(8)])


def pick(value, at, axis=0):
    return lax.dynamic_index_in_dim(value, at, axis, keepdims=False)


def after(value, *others):
    return lax.optimization_barrier((value, *others))


def shards(acts, out_grads, basis, weight, first_moment, second_moment):
    rank_local, width = first_moment.shape
    rows, rank = basis.shape
    tokens = acts.shape[0]
    x, y, zh, zl, core = (lax.axis_index(a) for a in ("x", "y", "zh", "zl", "core"))

    with jax.named_scope("tiles"):
        tile = lax.dynamic_slice_in_dim(basis, y * (rank // 4), rank // 4, 1)
        below, above = along_z(tile, 1), along_z(tile, 7)
    with jax.named_scope("project"):
        partial_t = lax.dot_general(
            basis, acts, (((0,), (1,)), ((), ())), preferred_element_type=F32
        ).reshape(4, 2, rank_local, tokens)
    partial_t, below, above = after(partial_t, below, above)
    with jax.named_scope("tiles"):
        second = along_z(below, 1)
        low = jnp.stack([tile, below])
    with jax.named_scope("project"):
        got = swap(pick(partial_t, 1 - core, 1).astype(BF), "core")
        mixed = pick(partial_t, core, 1) + got.astype(F32)
    mixed, second = after(mixed, second)
    with jax.named_scope("tiles_y"):
        down_low, up_low = around(low, 1, "y"), around(low, 3, "y")
        high = jnp.stack([second, above])
    with jax.named_scope("project"):
        total = pick(mixed, zl)
        for r in range(1, 4):
            total = total + around(pick(mixed, (zl + r) % 4).astype(BF), r).astype(F32)
        ranks_t = total.astype(BF)
    ranks_t, down_low, up_low, weight = after(ranks_t, down_low, up_low, weight)
    with jax.named_scope("weight_hops"):
        hops = [weight, around(weight, 1)]
    with jax.named_scope("tiles_y"):
        down_high, up_high = around(high, 1, "y"), around(high, 3, "y")
    with jax.named_scope("grad"):
        blocks = grad_blocks(ranks_t, out_grads, width)
    blocks, hops[1], down_high, up_high = after(blocks, hops[1], down_high, up_high)
    with jax.named_scope("grad"):
        parts = lax.all_to_all(blocks.reshape(16, 2, rank_local, width), ("x", "y"), 0, 0)
    with jax.named_scope("tiles_y"):
        far_low, far_high = around(down_low, 1, "y"), around(up_high, 3, "y")
        plane = jnp.concatenate([low, high])
        bases = [plane, down_low, down_high, far_low, far_high, up_low, up_high]
    with jax.named_scope("weight_hops"):
        hops.append(around(hops[1], 1))
        hops.append(around(hops[2], 1))
    with jax.named_scope("other_core"):
        other_bases = [swap(b, "core") for b in bases]
        others = [swap(h, "core") for h in hops[:3]]
    parts, hops[3], *swapped = after(parts, hops[3], *other_bases, *others)
    other_bases, others = swapped[:7], swapped[7:]
    with jax.named_scope("grad"):
        halves = jnp.sum(parts.astype(F32), axis=0)
        grad = pick(halves, zh) + swap(pick(halves, 1 - zh).astype(BF), "zh").astype(F32)

    with jax.named_scope("adam"):
        new_first = 0.9 * first_moment + 0.1 * grad
        new_second = 0.999 * second_moment + 0.001 * grad * grad
        direction = (
            new_first / first_fix / (jnp.sqrt(new_second / second_fix) + 1e-08)
        ).astype(BF)

    with jax.named_scope("other_core"):
        others.append(swap(hops[3], "core"))
    with jax.named_scope("lift"):
        theirs = swap(direction, "core")
        pair = jnp.where(
            core == 0,
            jnp.concatenate([direction, theirs]),
            jnp.concatenate([theirs, direction]),
        )
        pieces = [pair] + [around(pair, r) for r in range(1, 4)]
        where = jnp.stack([y, zl, core]).astype(jnp.int32)
        new_weight = lift(where, pieces, hops + others, bases + other_bases)
    return (new_weight, new_first, new_second)


def solution(mesh):
    split = Mesh(mesh.devices.reshape(4, 4, 2, 4, 2), DP + FSDP)
    placed = (
        P(DP, FSDP),
        P(DP, None),
        P(FSDP, None),
        P(FSDP, DP),
        P(FSDP, DP),
        P(FSDP, DP),
    )
    return jax.shard_map(
        shards,
        mesh=split,
        in_specs=placed,
        out_specs=(P(None, DP), P(FSDP, DP), P(FSDP, DP)),
        check_vma=False,
    )
```

```python
import jax
import jax.numpy as jnp
from jax import lax
from jax.experimental import pallas as pl
from jax.experimental.pallas import tpu as pltpu
from jax.sharding import Mesh, PartitionSpec as P

first_fix = 0.99997343860111
second_fix = 0.0952078528

DP = ("x", "y", "zh")
FSDP = ("zl", "core")
BF = jnp.bfloat16
F32 = jnp.float32


def grad_kernel(ranks_ref, grads_ref, out_ref):
    product = jnp.dot(ranks_ref[...], grads_ref[...], preferred_element_type=F32).astype(BF)
    width = out_ref.shape[-1]
    for i in range(out_ref.shape[0]):
        out_ref[i] = product[:, i * width : (i + 1) * width]


def grad_blocks(ranks, out_grads, width):
    rank_local, tokens = ranks.shape
    blocks = out_grads.shape[1] // width
    step = 8
    return pl.pallas_call(
        grad_kernel,
        grid=(blocks // step,),
        in_specs=[
            pl.BlockSpec((rank_local, tokens), lambda j: (0, 0)),
            pl.BlockSpec((tokens, step * width), lambda j: (0, j)),
        ],
        out_specs=pl.BlockSpec((step, rank_local, width), lambda j: (j, 0, 0)),
        out_shape=jax.ShapeDtypeStruct((blocks, rank_local, width), BF),
        compiler_params=pltpu.CompilerParams(vmem_limit_bytes=60 * 2**20),
        cost_estimate=pl.CostEstimate(
            flops=8 * rank_local * tokens * blocks * width,
            bytes_accessed=2 * tokens * blocks * width,
            transcendentals=0,
        ),
    )(ranks, out_grads)


def lift_kernel(where_ref, *refs):
    pieces, weights, bases, rest = refs[:4], refs[4:12], refs[12:22], refs[22:]
    out_ref, dirs, old, base, done, in_sems, out_sems = rest
    color, zl, core = (where_ref[i] for i in range(3))
    pair = pieces[0].shape[0]
    rows = old.shape[2]
    lanes = base.shape[3] // 4
    loads = []
    for k in range(2):
        plane, right, far_low, far_high, left = bases[5 * k : 5 * k + 5]
        for z in range(4):
            far = (far_low, far_high)[z // 2].at[z % 2]
            sources = [plane.at[z], right.at[z], far, left.at[z]]
            group = [pltpu.make_async_copy(weights[4 * k + z], old.at[k, z], in_sems.at[k, z, 4])]
            for q, source in enumerate(sources):
                group.append(
                    pltpu.make_async_copy(
                        source,
                        base.at[k, z, :, q * lanes : (q + 1) * lanes],
                        in_sems.at[k, z, q],
                    )
                )
            for copy in group:
                copy.start()
            loads.append(group)
    for r, piece in enumerate(pieces):
        at = lax.rem(zl - r - color + 8, 4) * pair
        dirs[pl.ds(pl.multiple_of(at, pair), pair), :] = piece[...]
    stores = []
    for k in range(2):
        for z in range(4):
            for copy in loads[4 * k + z]:
                copy.wait()
            lifted = jnp.dot(base[k, z], dirs[...], preferred_element_type=F32)
            done[k, z] = (old[k, z].astype(F32) - 8.0 * lifted).astype(BF)
            owner = core if k == 0 else 1 - core
            at = (lax.rem(zl - z + 4, 4) * 2 + owner) * rows
            copy = pltpu.make_async_copy(
                done.at[k, z],
                out_ref.at[pl.ds(pl.multiple_of(at, rows), rows)],
                out_sems.at[k, z],
            )
            copy.start()
            stores.append(copy)
    for copy in stores:
        copy.wait()


def lift(where, pieces, weights, bases):
    rows, width = weights[0].shape
    pair = pieces[0].shape[0]
    lanes = bases[0].shape[2]
    anywhere = pl.BlockSpec(memory_space=pl.ANY)
    return pl.pallas_call(
        lift_kernel,
        in_specs=[pl.BlockSpec(memory_space=pltpu.SMEM)]
        + [pl.BlockSpec(memory_space=pltpu.VMEM)] * 4
        + [anywhere] * 18,
        out_specs=anywhere,
        scratch_shapes=[
            pltpu.VMEM((4 * pair, width), BF),
            pltpu.VMEM((2, 4, rows, width), BF),
            pltpu.VMEM((2, 4, rows, 4 * lanes), BF),
            pltpu.VMEM((2, 4, rows, width), BF),
            pltpu.SemaphoreType.DMA((2, 4, 5)),
            pltpu.SemaphoreType.DMA((2, 4)),
        ],
        out_shape=jax.ShapeDtypeStruct((8 * rows, width), BF),
        compiler_params=pltpu.CompilerParams(vmem_limit_bytes=56 * 2**20),
        cost_estimate=pl.CostEstimate(
            flops=16 * rows * 4 * pair * width,
            bytes_accessed=16 * rows * (2 * width + 4 * pair),
            transcendentals=0,
        ),
    )(where, *pieces, *weights, *bases)


def swap(value, axis):
    return lax.ppermute(value, axis, [(0, 1), (1, 0)])


def around(value, shift, axis="zl"):
    return lax.ppermute(value, axis, [(i, (i + shift) % 4) for i in range(4)])


def along_z(value, shift):
    return lax.ppermute(value, ("zh", "zl"), [(i, (i + shift) % 8) for i in range(8)])


def pick(value, at, axis=0):
    return lax.dynamic_index_in_dim(value, at, axis, keepdims=False)


def after(*values):
    return lax.optimization_barrier(values)


def shards(acts, out_grads, basis, weight, first_moment, second_moment):
    rank_local, width = first_moment.shape
    rows, rank = basis.shape
    tokens = acts.shape[0]
    x, y, zh, zl, core = (lax.axis_index(a) for a in ("x", "y", "zh", "zl", "core"))

    color = (x + 2 * y) % 4
    with jax.named_scope("tiles"):
        tile = lax.dynamic_slice_in_dim(basis, color * (rank // 4), rank // 4, 1)
        (tile,) = after(tile)
        below, above = along_z(tile, 1), along_z(tile, 7)
    with jax.named_scope("project"):
        partial_t = lax.dot_general(
            basis, acts, (((0,), (1,)), ((), ())), preferred_element_type=F32
        ).reshape(4, 2, rank_local, tokens)
    partial_t, below, above = after(partial_t, below, above)
    with jax.named_scope("project"):
        got = swap(pick(partial_t, 1 - core, 1).astype(BF), "core")
        mixed = pick(partial_t, core, 1) + got.astype(F32)
        got = [around(pick(mixed, (zl + r) % 4).astype(BF), r) for r in range(1, 4)]
    got[0], below, weight = after(got[0], below, weight)
    with jax.named_scope("weight_hops"):
        hops = [weight, around(weight, 1)]
    with jax.named_scope("tiles"):
        second = along_z(below, 1)
    with jax.named_scope("project"):
        total = pick(mixed, zl) + sum(part.astype(F32) for part in got)
        ranks_t = total.astype(BF)
    ranks_t, tile, below, second, above = after(ranks_t, tile, below, second, above)
    with jax.named_scope("tiles_xy"):
        plane = jnp.stack([tile, below, second, above])
        right, left = around(plane, 3, "x"), around(plane, 1, "x")
        far_low, far_high = around(plane[:2], 1, "y"), around(plane[2:], 3, "y")
    with jax.named_scope("grad"):
        blocks = grad_blocks(ranks_t, out_grads, width)
    blocks, weight, hops[1], *bases = after(
        blocks, weight, hops[1], plane, right, far_low, far_high, left
    )
    hops[0] = weight
    with jax.named_scope("grad"):
        parts = lax.all_to_all(blocks.reshape(16, 2, rank_local, width), ("x", "y"), 0, 0)
    with jax.named_scope("weight_hops"):
        hops.append(around(hops[1], 1))
        hops.append(around(hops[2], 1))
    hops[3], bases[2] = after(hops[3], bases[2])
    with jax.named_scope("other_core"):
        other_bases = [swap(b, "core") for b in bases]
        others = [swap(h, "core") for h in hops[:3]]
    parts, hops[3], *swapped = after(parts, hops[3], *other_bases, *others)
    other_bases, others = swapped[:5], swapped[5:]
    with jax.named_scope("grad"):
        halves = jnp.sum(parts.astype(F32), axis=0)
        grad = pick(halves, zh) + swap(pick(halves, 1 - zh).astype(BF), "zh").astype(F32)

    with jax.named_scope("adam"):
        new_first = 0.9 * first_moment + 0.1 * grad
        new_second = 0.999 * second_moment + 0.001 * grad * grad
        direction = (
            new_first / first_fix / (jnp.sqrt(new_second / second_fix) + 1e-08)
        ).astype(BF)

    with jax.named_scope("other_core"):
        others.append(swap(hops[3], "core"))
    with jax.named_scope("lift"):
        theirs = swap(direction, "core")
        pair = jnp.where(
            core == 0,
            jnp.concatenate([direction, theirs]),
            jnp.concatenate([theirs, direction]),
        )
        pieces = [pair] + [around(pair, r) for r in range(1, 4)]
        where = jnp.stack([color, zl, core]).astype(jnp.int32)
        new_weight = lift(where, pieces, hops + others, bases + other_bases)
    return (new_weight, new_first, new_second)


def solution(mesh):
    split = Mesh(mesh.devices.reshape(4, 4, 2, 4, 2), DP + FSDP)
    placed = (
        P(DP, FSDP),
        P(DP, None),
        P(FSDP, None),
        P(FSDP, DP),
        P(FSDP, DP),
        P(FSDP, DP),
    )
    return jax.shard_map(
        shards,
        mesh=split,
        in_specs=placed,
        out_specs=(P(None, DP), P(FSDP, DP), P(FSDP, DP)),
        check_vma=False,
    )
```

```python
import jax
import jax.numpy as jnp
from jax import lax
from jax.experimental import pallas as pl
from jax.experimental.pallas import tpu as pltpu
from jax.sharding import Mesh, PartitionSpec as P

first_fix = 0.99997343860111
second_fix = 0.0952078528

DP = ("x", "y", "zh")
FSDP = ("zl", "core")
BF = jnp.bfloat16
F32 = jnp.float32


def grad_kernel(ranks_ref, grads_ref, out_ref):
    product = jnp.dot(ranks_ref[...], grads_ref[...], preferred_element_type=F32).astype(BF)
    width = out_ref.shape[-1]
    for i in range(out_ref.shape[0]):
        out_ref[i] = product[:, i * width : (i + 1) * width]


def grad_blocks(ranks, out_grads, width):
    rank_local, tokens = ranks.shape
    blocks = out_grads.shape[1] // width
    step = 8
    return pl.pallas_call(
        grad_kernel,
        grid=(blocks // step,),
        in_specs=[
            pl.BlockSpec((rank_local, tokens), lambda j: (0, 0)),
            pl.BlockSpec((tokens, step * width), lambda j: (0, j)),
        ],
        out_specs=pl.BlockSpec((step, rank_local, width), lambda j: (j, 0, 0)),
        out_shape=jax.ShapeDtypeStruct((blocks, rank_local, width), BF),
        compiler_params=pltpu.CompilerParams(vmem_limit_bytes=60 * 2**20),
        cost_estimate=pl.CostEstimate(
            flops=8 * rank_local * tokens * blocks * width,
            bytes_accessed=2 * tokens * blocks * width,
            transcendentals=0,
        ),
    )(ranks, out_grads)


def lift_kernel(where_ref, *refs):
    pieces, weights, bases, rest = refs[:4], refs[4:12], refs[12:28], refs[28:]
    out_ref, dirs, old, base, done, in_sems, out_sems = rest
    color, zl, core = (where_ref[i] for i in range(3))
    pair = pieces[0].shape[0]
    rows = old.shape[2]
    lanes = base.shape[3] // 4
    loads = []
    for k in range(2):
        three, one = bases[8 * k : 8 * k + 4], bases[8 * k + 4 : 8 * k + 8]
        for z in range(4):
            sources = [b.at[0] for b in one] if z == 2 else [b.at[min(z, 2)] for b in three]
            group = [pltpu.make_async_copy(weights[4 * k + z], old.at[k, z], in_sems.at[k, z, 4])]
            for q, source in enumerate(sources):
                group.append(
                    pltpu.make_async_copy(
                        source,
                        base.at[k, z, :, q * lanes : (q + 1) * lanes],
                        in_sems.at[k, z, q],
                    )
                )
            for copy in group:
                copy.start()
            loads.append(group)
    for r, piece in enumerate(pieces):
        at = lax.rem(zl - r - color + 8, 4) * pair
        dirs[pl.ds(pl.multiple_of(at, pair), pair), :] = piece[...]
    stores = []
    for k in range(2):
        for z in range(4):
            for copy in loads[4 * k + z]:
                copy.wait()
            lifted = jnp.dot(base[k, z], dirs[...], preferred_element_type=F32)
            done[k, z] = (old[k, z].astype(F32) - 8.0 * lifted).astype(BF)
            owner = core if k == 0 else 1 - core
            at = (lax.rem(zl - z + 4, 4) * 2 + owner) * rows
            copy = pltpu.make_async_copy(
                done.at[k, z],
                out_ref.at[pl.ds(pl.multiple_of(at, rows), rows)],
                out_sems.at[k, z],
            )
            copy.start()
            stores.append(copy)
    for copy in stores:
        copy.wait()


def lift(where, pieces, weights, bases):
    rows, width = weights[0].shape
    pair = pieces[0].shape[0]
    lanes = bases[0].shape[2]
    anywhere = pl.BlockSpec(memory_space=pl.ANY)
    return pl.pallas_call(
        lift_kernel,
        in_specs=[pl.BlockSpec(memory_space=pltpu.SMEM)]
        + [pl.BlockSpec(memory_space=pltpu.VMEM)] * 4
        + [anywhere] * 24,
        out_specs=anywhere,
        scratch_shapes=[
            pltpu.VMEM((4 * pair, width), BF),
            pltpu.VMEM((2, 4, rows, width), BF),
            pltpu.VMEM((2, 4, rows, 4 * lanes), BF),
            pltpu.VMEM((2, 4, rows, width), BF),
            pltpu.SemaphoreType.DMA((2, 4, 5)),
            pltpu.SemaphoreType.DMA((2, 4)),
        ],
        out_shape=jax.ShapeDtypeStruct((8 * rows, width), BF),
        compiler_params=pltpu.CompilerParams(vmem_limit_bytes=56 * 2**20),
        cost_estimate=pl.CostEstimate(
            flops=16 * rows * 4 * pair * width,
            bytes_accessed=16 * rows * (2 * width + 4 * pair),
            transcendentals=0,
        ),
    )(where, *pieces, *weights, *bases)


def swap(value, axis):
    return lax.ppermute(value, axis, [(0, 1), (1, 0)])


def around(value, shift, axis="zl"):
    return lax.ppermute(value, axis, [(i, (i + shift) % 4) for i in range(4)])


def along_z(value, shift):
    return lax.ppermute(value, ("zh", "zl"), [(i, (i + shift) % 8) for i in range(8)])


def pick(value, at, axis=0):
    return lax.dynamic_index_in_dim(value, at, axis, keepdims=False)


def after(value, *others):
    return lax.optimization_barrier((value, *others))


def shards(acts, out_grads, basis, weight, first_moment, second_moment):
    rank_local, width = first_moment.shape
    rows, rank = basis.shape
    tokens = acts.shape[0]
    x, y, zh, zl, core = (lax.axis_index(a) for a in ("x", "y", "zh", "zl", "core"))

    color = (x + 2 * y) % 4
    with jax.named_scope("tiles"):
        tile = lax.dynamic_slice_in_dim(basis, color * (rank // 4), rank // 4, 1)
        (tile,) = after(tile)
        below, above = along_z(tile, 1), along_z(tile, 7)
    with jax.named_scope("project"):
        partial_t = lax.dot_general(
            basis, acts, (((0,), (1,)), ((), ())), preferred_element_type=F32
        ).reshape(4, 2, rank_local, tokens)
    partial_t, below, above = after(partial_t, below, above)
    with jax.named_scope("project"):
        got = swap(pick(partial_t, 1 - core, 1).astype(BF), "core")
        mixed = pick(partial_t, core, 1) + got.astype(F32)
        got = [around(pick(mixed, (zl + r) % 4).astype(BF), r) for r in range(1, 4)]
    got[0], tile, below, above, weight = after(got[0], tile, below, above, weight)
    with jax.named_scope("weight_hops"):
        hops = [weight, around(weight, 1)]
    with jax.named_scope("tiles"):
        second = along_z(below, 1)
        own = jnp.stack([tile, below, above])
    with jax.named_scope("tiles_xy"):
        right, left = around(own, 3, "x"), around(own, 1, "x")
    with jax.named_scope("project"):
        total = pick(mixed, zl) + sum(part.astype(F32) for part in got)
        ranks_t = total.astype(BF)
    ranks_t, own, second = after(ranks_t, own, second)
    with jax.named_scope("tiles_xy"):
        far = around(own, 1, "y")
    with jax.named_scope("grad"):
        blocks = grad_blocks(ranks_t, out_grads, width)
    blocks, second, weight, hops[1], *three = after(
        blocks, second, weight, hops[1], own, right, far, left
    )
    hops[0] = weight
    with jax.named_scope("grad"):
        parts = lax.all_to_all(blocks.reshape(16, 2, rank_local, width), ("x", "y"), 0, 0)
    with jax.named_scope("weight_hops"):
        hops.append(around(hops[1], 1))
        hops.append(around(hops[2], 1))
    with jax.named_scope("tiles_xy"):
        second = second[None]
        one = [second, around(second, 3, "x"), around(second, 3, "y"), around(second, 1, "x")]
    hops[3], one[0] = after(hops[3], one[0])
    bases = three + one
    with jax.named_scope("other_core"):
        other_bases = [swap(b, "core") for b in bases]
        others = [swap(h, "core") for h in hops[:3]]
    parts, hops[3], *swapped = after(parts, hops[3], *other_bases, *others)
    other_bases, others = swapped[:8], swapped[8:]
    with jax.named_scope("grad"):
        halves = jnp.sum(parts.astype(F32), axis=0)
        grad = pick(halves, zh) + swap(pick(halves, 1 - zh).astype(BF), "zh").astype(F32)

    with jax.named_scope("adam"):
        new_first = 0.9 * first_moment + 0.1 * grad
        new_second = 0.999 * second_moment + 0.001 * grad * grad
        direction = (
            new_first / first_fix / (jnp.sqrt(new_second / second_fix) + 1e-08)
        ).astype(BF)

    with jax.named_scope("other_core"):
        others.append(swap(hops[3], "core"))
    with jax.named_scope("lift"):
        theirs = swap(direction, "core")
        pair = jnp.where(
            core == 0,
            jnp.concatenate([direction, theirs]),
            jnp.concatenate([theirs, direction]),
        )
        pieces = [pair] + [around(pair, r) for r in range(1, 4)]
        where = jnp.stack([color, zl, core]).astype(jnp.int32)
        new_weight = lift(where, pieces, hops + others, bases + other_bases)
    return (new_weight, new_first, new_second)


def solution(mesh):
    split = Mesh(mesh.devices.reshape(4, 4, 2, 4, 2), DP + FSDP)
    placed = (
        P(DP, FSDP),
        P(DP, None),
        P(FSDP, None),
        P(FSDP, DP),
        P(FSDP, DP),
        P(FSDP, DP),
    )
    return jax.shard_map(
        shards,
        mesh=split,
        in_specs=placed,
        out_specs=(P(None, DP), P(FSDP, DP), P(FSDP, DP)),
        check_vma=False,
    )
```

```python
import jax
import jax.numpy as jnp
from jax import lax
from jax.experimental import pallas as pl
from jax.experimental.pallas import tpu as pltpu
from jax.sharding import Mesh, PartitionSpec as P

first_fix = 0.99997343860111
second_fix = 0.0952078528

DP = ("x", "y", "zh")
FSDP = ("zl", "core")
BF = jnp.bfloat16
F32 = jnp.float32


def grad_kernel(ranks_ref, grads_ref, out_ref):
    product = jnp.dot(ranks_ref[...], grads_ref[...], preferred_element_type=F32).astype(BF)
    width = out_ref.shape[-1]
    for i in range(out_ref.shape[0]):
        out_ref[i] = product[:, i * width : (i + 1) * width]


def grad_blocks(ranks, out_grads, width):
    rank_local, tokens = ranks.shape
    blocks = out_grads.shape[1] // width
    step = 8
    return pl.pallas_call(
        grad_kernel,
        grid=(blocks // step,),
        in_specs=[
            pl.BlockSpec((rank_local, tokens), lambda j: (0, 0)),
            pl.BlockSpec((tokens, step * width), lambda j: (0, j)),
        ],
        out_specs=pl.BlockSpec((step, rank_local, width), lambda j: (j, 0, 0)),
        out_shape=jax.ShapeDtypeStruct((blocks, rank_local, width), BF),
        compiler_params=pltpu.CompilerParams(vmem_limit_bytes=60 * 2**20),
        cost_estimate=pl.CostEstimate(
            flops=8 * rank_local * tokens * blocks * width,
            bytes_accessed=2 * tokens * blocks * width,
            transcendentals=0,
        ),
    )(ranks, out_grads)


def lift_kernel(where_ref, *refs):
    pieces, weights, bases, rest = refs[:4], refs[4:12], refs[12:30], refs[30:]
    out_ref, dirs, old, base, done, in_sems, out_sems = rest
    color, zl, core = (where_ref[i] for i in range(3))
    pair = pieces[0].shape[0]
    rows = old.shape[2]
    lanes = base.shape[3] // 4
    loads = []
    for k in range(2):
        own, right, far_low, far_high, left, *one = bases[9 * k : 9 * k + 9]
        for z in range(4):
            at = min(z, 2)
            far = far_low.at[z] if z < 2 else far_high.at[0]
            three = [own.at[at], right.at[at], far, left.at[at]]
            sources = [b.at[0] for b in one] if z == 2 else three
            group = [pltpu.make_async_copy(weights[4 * k + z], old.at[k, z], in_sems.at[k, z, 4])]
            for q, source in enumerate(sources):
                group.append(
                    pltpu.make_async_copy(
                        source,
                        base.at[k, z, :, q * lanes : (q + 1) * lanes],
                        in_sems.at[k, z, q],
                    )
                )
            for copy in group:
                copy.start()
            loads.append(group)
    for r, piece in enumerate(pieces):
        at = lax.rem(zl - r - color + 8, 4) * pair
        dirs[pl.ds(pl.multiple_of(at, pair), pair), :] = piece[...]
    stores = []
    for k in range(2):
        for z in range(4):
            for copy in loads[4 * k + z]:
                copy.wait()
            lifted = jnp.dot(base[k, z], dirs[...], preferred_element_type=F32)
            done[k, z] = (old[k, z].astype(F32) - 8.0 * lifted).astype(BF)
            owner = core if k == 0 else 1 - core
            at = (lax.rem(zl - z + 4, 4) * 2 + owner) * rows
            copy = pltpu.make_async_copy(
                done.at[k, z],
                out_ref.at[pl.ds(pl.multiple_of(at, rows), rows)],
                out_sems.at[k, z],
            )
            copy.start()
            stores.append(copy)
    for copy in stores:
        copy.wait()


def lift(where, pieces, weights, bases):
    rows, width = weights[0].shape
    pair = pieces[0].shape[0]
    lanes = bases[0].shape[2]
    anywhere = pl.BlockSpec(memory_space=pl.ANY)
    return pl.pallas_call(
        lift_kernel,
        in_specs=[pl.BlockSpec(memory_space=pltpu.SMEM)]
        + [pl.BlockSpec(memory_space=pltpu.VMEM)] * 4
        + [anywhere] * 26,
        out_specs=anywhere,
        scratch_shapes=[
            pltpu.VMEM((4 * pair, width), BF),
            pltpu.VMEM((2, 4, rows, width), BF),
            pltpu.VMEM((2, 4, rows, 4 * lanes), BF),
            pltpu.VMEM((2, 4, rows, width), BF),
            pltpu.SemaphoreType.DMA((2, 4, 5)),
            pltpu.SemaphoreType.DMA((2, 4)),
        ],
        out_shape=jax.ShapeDtypeStruct((8 * rows, width), BF),
        compiler_params=pltpu.CompilerParams(vmem_limit_bytes=56 * 2**20),
        cost_estimate=pl.CostEstimate(
            flops=16 * rows * 4 * pair * width,
            bytes_accessed=16 * rows * (2 * width + 4 * pair),
            transcendentals=0,
        ),
    )(where, *pieces, *weights, *bases)


def swap(value, axis):
    return lax.ppermute(value, axis, [(0, 1), (1, 0)])


def around(value, shift, axis="zl"):
    return lax.ppermute(value, axis, [(i, (i + shift) % 4) for i in range(4)])


def along_z(value, shift):
    return lax.ppermute(value, ("zh", "zl"), [(i, (i + shift) % 8) for i in range(8)])


def pick(value, at, axis=0):
    return lax.dynamic_index_in_dim(value, at, axis, keepdims=False)


def after(value, *others):
    return lax.optimization_barrier((value, *others))


def shards(acts, out_grads, basis, weight, first_moment, second_moment):
    rank_local, width = first_moment.shape
    rows, rank = basis.shape
    tokens = acts.shape[0]
    x, y, zh, zl, core = (lax.axis_index(a) for a in ("x", "y", "zh", "zl", "core"))

    color = (x + 2 * y) % 4
    with jax.named_scope("tiles"):
        tile = lax.dynamic_slice_in_dim(basis, color * (rank // 4), rank // 4, 1)
        (tile,) = after(tile)
        below, above = along_z(tile, 1), along_z(tile, 7)
    with jax.named_scope("project"):
        partial_t = lax.dot_general(
            basis, acts, (((0,), (1,)), ((), ())), preferred_element_type=F32
        ).reshape(4, 2, rank_local, tokens)
    partial_t, below, above = after(partial_t, below, above)
    with jax.named_scope("project"):
        got = swap(pick(partial_t, 1 - core, 1).astype(BF), "core")
        mixed = pick(partial_t, core, 1) + got.astype(F32)
        got = [around(pick(mixed, (zl + r) % 4).astype(BF), r) for r in range(1, 4)]
    got[0], tile, below, above, weight = after(got[0], tile, below, above, weight)
    with jax.named_scope("weight_hops"):
        hops = [weight, around(weight, 1)]
    with jax.named_scope("tiles"):
        second = along_z(below, 1)
        own = jnp.stack([tile, below, above])
    with jax.named_scope("tiles_xy"):
        right, left = around(own, 3, "x"), around(own, 1, "x")
    with jax.named_scope("project"):
        total = pick(mixed, zl) + sum(part.astype(F32) for part in got)
        ranks_t = total.astype(BF)
    ranks_t, own, second = after(ranks_t, own, second)
    with jax.named_scope("tiles_xy"):
        far_low, far_high = around(own[:2], 1, "y"), around(own[2:], 3, "y")
    with jax.named_scope("grad"):
        blocks = grad_blocks(ranks_t, out_grads, width)
    blocks, second, weight, hops[1], *three = after(
        blocks, second, weight, hops[1], own, right, far_low, far_high, left
    )
    hops[0] = weight
    with jax.named_scope("grad"):
        parts = lax.all_to_all(blocks.reshape(16, 2, rank_local, width), ("x", "y"), 0, 0)
    with jax.named_scope("weight_hops"):
        hops.append(around(hops[1], 1))
        hops.append(around(hops[2], 1))
    with jax.named_scope("tiles_xy"):
        second = second[None]
        one = [second, around(second, 3, "x"), around(second, 3, "y"), around(second, 1, "x")]
    hops[3], one[0] = after(hops[3], one[0])
    bases = three + one
    with jax.named_scope("other_core"):
        other_bases = [swap(b, "core") for b in bases]
        others = [swap(h, "core") for h in hops[:3]]
    parts, hops[3], *swapped = after(parts, hops[3], *other_bases, *others)
    other_bases, others = swapped[:9], swapped[9:]
    with jax.named_scope("grad"):
        halves = jnp.sum(parts.astype(F32), axis=0)
        grad = pick(halves, zh) + swap(pick(halves, 1 - zh).astype(BF), "zh").astype(F32)

    with jax.named_scope("adam"):
        new_first = 0.9 * first_moment + 0.1 * grad
        new_second = 0.999 * second_moment + 0.001 * grad * grad
        direction = (
            new_first / first_fix / (jnp.sqrt(new_second / second_fix) + 1e-08)
        ).astype(BF)

    with jax.named_scope("other_core"):
        others.append(swap(hops[3], "core"))
    with jax.named_scope("lift"):
        theirs = swap(direction, "core")
        pair = jnp.where(
            core == 0,
            jnp.concatenate([direction, theirs]),
            jnp.concatenate([theirs, direction]),
        )
        pieces = [pair] + [around(pair, r) for r in range(1, 4)]
        where = jnp.stack([color, zl, core]).astype(jnp.int32)
        new_weight = lift(where, pieces, hops + others, bases + other_bases)
    return (new_weight, new_first, new_second)


def solution(mesh):
    split = Mesh(mesh.devices.reshape(4, 4, 2, 4, 2), DP + FSDP)
    placed = (
        P(DP, FSDP),
        P(DP, None),
        P(FSDP, None),
        P(FSDP, DP),
        P(FSDP, DP),
        P(FSDP, DP),
    )
    return jax.shard_map(
        shards,
        mesh=split,
        in_specs=placed,
        out_specs=(P(None, DP), P(FSDP, DP), P(FSDP, DP)),
        check_vma=False,
    )
```
